32 devices in a mesh: seq: 8 (over z, x), head: 4 (over y, core).
Axes of the slice: x: 2, y: 2, z: 4, core: 2. Of those that a mesh axis runs over, the one named last changes fastest.
Arguments:
- hidden: float32 [16384, 768], P('seq'), may hold values from -6 to 6
- doc_starts: int32 [5], replicated, may hold values from 0 to 16383, as said below
- norm_gain: float32 [2, 768], replicated, may hold values from 0.5 to 1.5
- w_gate: bfloat16 [2, 768, 1536], P(None, None, 'head'), may hold values from -0.21875 to 0.21875
- w_value: bfloat16 [2, 768, 1536], P(None, None, 'head'), may hold values from -0.21875 to 0.21875
- w_state: bfloat16 [2, 768, 256], replicated, may hold values from -0.21875 to 0.21875
- w_step: bfloat16 [2, 768, 24], P(None, None, 'head'), may hold values from -0.21875 to 0.21875
- conv_value: float32 [2, 4, 1536], P(None, None, 'head'), may hold values from -3 to 3
- conv_state: float32 [2, 4, 256], replicated, may hold values from -3 to 3
- bias_value: float32 [2, 1536], P(None, 'head'), may hold values from -2.5 to 2.5
- bias_state: float32 [2, 256], replicated, may hold values from -2.5 to 2.5
- step_bias: float32 [2, 24], P(None, 'head'), may hold values from -1 to 1
- a_log: float32 [2, 24], P(None, 'head')
- skip_gain: float32 [2, 24], P(None, 'head'), may hold values from 0.5 to 1.5
- mix_gain: float32 [2, 1536], P(None, 'head'), may hold values from 0.5 to 1.5
- w_out: bfloat16 [2, 1536, 768], P(None, 'head'), may hold values from -0.15625 to 0.15625
- cotangent: float32 [16384, 768], P('seq'), may hold values from -6 to 6
Outputs:
- result: float32 [16384, 768], P('seq')
- grad_hidden: float32 [16384, 768], P('seq')
- grad_norm_gain: float32 [2, 768], replicated
- grad_w_gate: float32 [2, 768, 1536], P(None, None, 'head')
- grad_w_value: float32 [2, 768, 1536], P(None, None, 'head')
- grad_w_state: float32 [2, 768, 256], replicated
- grad_w_step: float32 [2, 768, 24], P(None, None, 'head')
- grad_conv_value: float32 [2, 4, 1536], P(None, None, 'head')
- grad_conv_state: float32 [2, 4, 256], replicated
- grad_bias_value: float32 [2, 1536], P(None, 'head')
- grad_bias_state: float32 [2, 256], replicated
- grad_step_bias: float32 [2, 24], P(None, 'head')
- grad_a_log: float32 [2, 24], P(None, 'head')
- grad_skip_gain: float32 [2, 24], P(None, 'head')
- grad_mix_gain: float32 [2, 1536], P(None, 'head')
- grad_w_out: float32 [2, 1536, 768], P(None, 'head')
The draws below stay inside these ranges and needn't reach their ends.
Inputs may be any that keep to these rules, and one draw needn't show every extreme that they name: `doc_starts`: 5 increasing positions, the first 0 and the last 16383; a document runs from its start to the next start, the last one to the end of the sequence.
All inputs are finite; a program needn't handle non-finite values.
Results may differ from the reference program's by a relative error of at most 0.024.
The reference program's roundings to bfloat16 on the way count: a program that leaves them out, or rounds other values in their place, can miss the bound.
Values may be sent and summed in bfloat16 or wider, within the bound.
No kernel may reach another device: no remote copies, remote signals or barrier semaphores. Data moves between devices by JAX's collectives and lax.ppermute only.
A program may use at most 256 MiB of HBM per device.

```python
import math
from functools import partial
import jax
import jax.numpy as jnp
from jax import lax

D = 768
HEADS = 24
HEAD_DIM = 64
STATE = 128
KERNEL = 4
GROUP = 256
LAYERS = 2
TOK_DEV = 2048
INNER = 1536
TOKENS = 16384


def draw_doc_starts(key, part):
    key = jax.random.fold_in(key, 23)
    keys = jax.random.split(key, 3)
    opening = jax.random.randint(keys[0], (), 2, TOK_DEV)
    early = jax.random.randint(keys[1], (), 1, opening)
    margin = jax.random.randint(keys[2], (), 2, TOK_DEV + 1)
    closing = TOKENS - margin
    late = jnp.full((), TOKENS - 1, jnp.int32)
    return jnp.stack([jnp.zeros((), jnp.int32), early, opening, closing, late]).astype(jnp.int32)


def draw_a_log(key, part):
    key = jax.random.fold_in(key, 11)
    keys = jax.random.split(key, 3)
    ranking = jax.random.permutation(keys[0], LAYERS * HEADS).reshape(LAYERS, HEADS)
    keep_count = LAYERS * HEADS // 2
    slow = jax.random.uniform(keys[1], (LAYERS, HEADS), jnp.float32, math.log(0.3 / TOKENS), math.log(2.0 / TOKENS))
    quick = jax.random.uniform(keys[2], (LAYERS, HEADS), jnp.float32, math.log(0.01), math.log(0.06))
    return jnp.where(ranking < keep_count, slow, quick).astype(jnp.float32)


def level_of(rng, shape, cuts, smallest, high):
    level, own = 1.0, jax.random.fold_in(rng, 6)
    for axis_at, parts in cuts:
        draws = jnp.exp(jax.random.uniform(jax.random.fold_in(own, axis_at), (parts,), jnp.float32, smallest / len(cuts), high / len(cuts)))
        level = level * jnp.repeat(draws, shape[axis_at] // parts).reshape([-1 if axis == axis_at else 1 for axis in range(len(shape))])
    return level


def centred(own_key, extent, width, reach, cuts=(), kind=jnp.bfloat16):
    result = width * jax.random.normal(own_key, extent, jnp.float32)
    if cuts:
        result = result * level_of(own_key, extent, cuts, -0.22, 0.18)
    return jnp.clip(result, -reach, reach).astype(kind)


def setup_inputs(seed: int = 0) -> dict:
    arg_keys = jax.random.split(jax.random.key(seed), 18)
    return {
        "hidden": centred(arg_keys[0], (TOKENS, D), 1.0, 6.0, ((0, 8),), jnp.float32),
        "doc_starts": draw_doc_starts(jax.random.fold_in(arg_keys[17], 71), 0),
        "norm_gain": jnp.clip(1.0 + 0.1 * jax.random.normal(arg_keys[2], (LAYERS, D), jnp.float32), 0.5, 1.5),
        "w_gate": centred(arg_keys[3], (LAYERS, D, INNER), D ** -0.5, 0.21875, ((2, 4),)),
        "w_value": centred(arg_keys[4], (LAYERS, D, INNER), D ** -0.5, 0.21875, ((2, 4),)),
        "w_state": centred(arg_keys[5], (LAYERS, D, 2 * STATE), D ** -0.5, 0.21875),
        "w_step": centred(arg_keys[6], (LAYERS, D, HEADS), D ** -0.5, 0.21875, ((2, 4),)),
        "conv_value": centred(arg_keys[7], (LAYERS, KERNEL, INNER), KERNEL ** -0.5, 3.0, ((2, 4),), jnp.float32),
        "conv_state": centred(arg_keys[8], (LAYERS, KERNEL, 2 * STATE), KERNEL ** -0.5, 3.0, (), jnp.float32),
        "bias_value": centred(arg_keys[9], (LAYERS, INNER), 0.5, 2.5, ((1, 4),), jnp.float32),
        "bias_state": centred(arg_keys[10], (LAYERS, 2 * STATE), 0.5, 2.5, (), jnp.float32),
        "step_bias": jnp.clip(jax.random.uniform(arg_keys[11], (LAYERS, HEADS), jnp.float32, -1.0, 1.0) * level_of(arg_keys[11], (LAYERS, HEADS), ((1, 4),), -0.4, 0.0), -1.0, 1.0),
        "a_log": draw_a_log(jax.random.fold_in(arg_keys[17], 71), 0),
        "skip_gain": jnp.clip(0.5 + 1.0 * jax.random.uniform(arg_keys[13], (LAYERS, HEADS), jnp.float32) ** level_of(arg_keys[13], (LAYERS, HEADS), ((1, 4),), -0.2, 0.2), 0.5, 1.5),
        "mix_gain": jnp.clip(1.0 + 0.1 * jax.random.normal(arg_keys[14], (LAYERS, INNER), jnp.float32), 0.5, 1.5),
        "w_out": centred(arg_keys[15], (LAYERS, INNER, D), INNER ** -0.5, 0.15625, ((1, 4),)),
        "cotangent": centred(arg_keys[16], (TOKENS, D), 1.0, 6.0, ((0, 8),), jnp.float32),
    }


EPS = 1e-05
HIGH = lax.Precision.HIGHEST

@jax.custom_vjp
def low(v):
    return lax.optimization_barrier(v.astype(jnp.bfloat16)).astype(jnp.float32)

@jax.custom_vjp
def low_back(v):
    return v

def low_keep(v):
    return (low(v), None)

def low_pass(kept, grad):
    return (grad,)

def back_keep(v):
    return (v, None)

def back_low(kept, grad):
    return (low(grad),)
low.defvjp(low_keep, low_pass)
low_back.defvjp(back_keep, back_low)

def matmul(left, right):
    return jnp.dot(left, right, precision=HIGH, preferred_element_type=jnp.float32)

def rms_scale(value):
    return value * lax.rsqrt(lax.optimization_barrier(jnp.mean(value * value, axis=-1, keepdims=True)) + EPS)

def segment_of(starts, positions):
    return lax.optimization_barrier(jnp.sum((starts[None, :] <= positions[:, None]).astype(jnp.int32), axis=1)) - 1

def causal_conv(padded, seg_pad, weight, bias):
    taps_count = weight.shape[0]
    length = padded.shape[0] - taps_count + 1
    seg_here = seg_pad[taps_count - 1:]
    total = jnp.zeros((length, padded.shape[1]), jnp.float32) + bias[None, :]
    for offset in range(taps_count):
        same_doc = (seg_pad[offset:offset + length] == seg_here).astype(jnp.float32)[:, None]
        total = total + weight[offset][None, :] * padded[offset:offset + length] * same_doc
    return total

def step_rates(raw, bias, log_rate):
    step = jax.nn.softplus(raw + bias[None, :])
    return (step, -step * jnp.exp(log_rate)[None, :])

def block_step(state, block):
    values, b_proj, c_proj, step, rate, seg, fresh = block
    block_len = values.shape[0]
    order_ids = jnp.arange(block_len)
    cumulative = jnp.cumsum(rate, axis=0)
    paired = (order_ids[:, None] >= order_ids[None, :]) & (seg[:, None] == seg[None, :])
    paired3 = paired[:, :, None]
    spread = cumulative[:, None, :] - cumulative[None, :, :]
    decay = jnp.where(paired3, jnp.exp(jnp.where(paired3, spread, 0.0)), 0.0)
    scores = matmul(c_proj, b_proj.T)
    scaled = values * step[:, :, None]
    inner_part = jnp.einsum('tsh,shp->thp', scores[:, :, None] * decay, scaled, precision=HIGH)
    alive = (jnp.cumsum(fresh) == 0).astype(jnp.float32)
    enter = jnp.exp(cumulative) * alive[:, None]
    carried = jnp.einsum('tn,hpn->thp', c_proj, state, precision=HIGH) * enter[:, :, None]
    tail = jnp.exp(cumulative[-1][None, :] - cumulative) * (seg == seg[-1]).astype(jnp.float32)[:, None]
    added = jnp.einsum('sh,shp,sn->hpn', tail, scaled, b_proj, precision=HIGH)
    return (state * enter[-1][:, None, None] + added, inner_part + carried)

def ssd_run(state, values, b_proj, c_proj, step, rate, seg, fresh):
    blocks_count = values.shape[0] // GROUP
    head_count = values.shape[1]
    head_width = values.shape[2]
    state_width = b_proj.shape[1]
    blocks = (values.reshape(blocks_count, GROUP, head_count, head_width), b_proj.reshape(blocks_count, GROUP, state_width), c_proj.reshape(blocks_count, GROUP, state_width), step.reshape(blocks_count, GROUP, head_count), rate.reshape(blocks_count, GROUP, head_count), seg.reshape(blocks_count, GROUP), fresh.reshape(blocks_count, GROUP))
    final_state, outputs = lax.scan(jax.checkpoint(block_step), state, blocks)
    return (final_state, outputs.reshape(blocks_count * GROUP, head_count, head_width))

def mamba_layer(hidden, weights, seg_pad, fresh):
    gain, w_gate, w_value, w_state, w_step, conv_value, conv_state, bias_value, bias_state, step_bias, a_log, skip_gain, mix_gain, w_out = weights
    tokens = hidden.shape[0]
    unit = low(rms_scale(hidden) * gain[None, :])
    proj = low(low_back(matmul(unit, jnp.concatenate([w_gate, w_value, w_step], axis=1))))
    state_proj = low(matmul(unit, w_state))
    conv_in = jnp.concatenate([proj[:, INNER:2 * INNER], state_proj], axis=1)
    padded = jnp.concatenate([jnp.zeros((KERNEL - 1, conv_in.shape[1]), jnp.float32), conv_in], axis=0)
    taps = jnp.concatenate([conv_value, conv_state], axis=1)
    biases = jnp.concatenate([bias_value, bias_state])
    post = low(jax.nn.silu(causal_conv(padded, seg_pad, taps, biases)))
    values = post[:, :INNER].reshape(tokens, HEADS, HEAD_DIM)
    b_proj = post[:, INNER:INNER + STATE]
    c_proj = post[:, INNER + STATE:]
    step, rate = step_rates(proj[:, 2 * INNER:], step_bias, a_log)
    start_state = jnp.zeros((HEADS, HEAD_DIM, STATE), jnp.float32)
    final_state, mixed = ssd_run(start_state, values, b_proj, c_proj, step, rate, seg_pad[KERNEL - 1:], fresh)
    mixed = (mixed + skip_gain[None, :, None] * values).reshape(tokens, INNER)
    gated = mixed * jax.nn.silu(proj[:, :INNER])
    normed = low(rms_scale(gated) * mix_gain[None, :])
    return hidden + low_back(matmul(normed, w_out))

def stacked_forward(hidden, weights, seg_pad, fresh):
    current = hidden
    for layer_index in range(LAYERS):
        current = mamba_layer(current, tuple((weight_stack[layer_index] for weight_stack in weights)), seg_pad, fresh)
    return current

def reference(hidden, doc_starts, norm_gain, w_gate, w_value, w_state, w_step, conv_value, conv_state, bias_value, bias_state, step_bias, a_log, skip_gain, mix_gain, w_out, cotangent):
    positions = jnp.arange(-(KERNEL - 1), TOKENS).astype(jnp.int32)
    seg_pad = segment_of(doc_starts.astype(jnp.int32), positions)
    fresh = jnp.any(doc_starts.astype(jnp.int32)[None, :] == positions[KERNEL - 1:, None], axis=1).astype(jnp.float32)
    weights = (norm_gain, w_gate.astype(jnp.float32), w_value.astype(jnp.float32), w_state.astype(jnp.float32), w_step.astype(jnp.float32), conv_value, conv_state, bias_value, bias_state, step_bias, a_log, skip_gain, mix_gain, w_out.astype(jnp.float32))
    output, backward = jax.vjp(partial(stacked_forward, seg_pad=seg_pad, fresh=fresh), hidden, weights)
    grad_hidden, grads = backward(cotangent)
    return (output, grad_hidden, grads[0], grads[1], grads[2], grads[3], grads[4], grads[5], grads[6], grads[7], grads[8], grads[9], grads[10], grads[11], grads[12], grads[13])
```

```python
from functools import partial

import jax
import jax.numpy as jnp
from jax import lax
from jax.experimental import pallas as pl
from jax.experimental.pallas import tpu as pltpu
from jax.sharding import PartitionSpec as P

GROUP = 256
LANES = 128
EPS = 1e-05
HIGH = lax.Precision.HIGHEST
BF = jnp.bfloat16
F32 = jnp.float32
FAR = -1e30


def up(width):
    return (width + LANES - 1) // LANES * LANES


def dot(left, right):
    return jnp.dot(left, right, preferred_element_type=F32)


def dot_t(left, right):
    return lax.dot_general(left, right, (((1,), (1,)), ((), ())), preferred_element_type=F32)


def t_dot(left, right):
    return lax.dot_general(left, right, (((0,), (0,)), ((), ())), preferred_element_type=F32)


def dot_high(left, right):
    return jnp.dot(left, right, precision=HIGH, preferred_element_type=F32)


def split(value, parts=2):
    pieces = []
    for _ in range(parts):
        pieces.append(value.astype(BF))
        value = value - pieces[-1].astype(F32)
    return pieces


def sum_dots(dot_of, left, right):
    most = max(len(left), len(right))
    pairs = [(i, j) for i in range(len(left)) for j in range(len(right)) if i + j < most]
    total = None
    for i, j in sorted(pairs, key=lambda pair: -sum(pair)):
        part = dot_of(left[i], right[j])
        total = part if total is None else total + part
    return total


def rms_scale(value):
    return value * lax.rsqrt(jnp.mean(value * value, axis=-1, keepdims=True) + EPS)


def causal_conv(rows, seg_pad, weight, bias):
    taps_count = weight.shape[0]
    length = rows.shape[0] - taps_count + 1
    seg_here = seg_pad[taps_count - 1 :]
    total = jnp.zeros((length, rows.shape[1]), F32) + bias[None, :]
    for offset in range(taps_count):
        same_doc = (seg_pad[offset : offset + length] == seg_here).astype(F32)[:, None]
        total = total + weight[offset][None, :] * rows[offset : offset + length] * same_doc
    return total


def lane_chunks(width):
    return [(start, min(LANES, width - start)) for start in range(0, width, LANES)]


def spread_heads(columns, inner, head_width):
    rows = columns.shape[0]
    lane = lax.broadcasted_iota(jnp.int32, (rows, LANES), 1)
    per = LANES // head_width
    pieces = []
    for start, width in lane_chunks(inner):
        first = start // head_width
        count = width // head_width
        piece = jnp.broadcast_to(columns[:, first : first + 1], (rows, LANES))
        for k in range(1, count):
            other = jnp.broadcast_to(columns[:, first + k : first + k + 1], (rows, LANES))
            piece = jnp.where(lane >= k * head_width, other, piece)
        pieces.append(piece[:, :width])
    return jnp.concatenate(pieces, axis=1)


def head_sums(values, head_width):
    inner = values.shape[1]
    row = lax.broadcasted_iota(jnp.int32, (inner, LANES), 0)
    column = lax.broadcasted_iota(jnp.int32, (inner, LANES), 1)
    member = jnp.where((row >= column * head_width) & (row < (column + 1) * head_width), 1.0, 0.0)
    return dot_high(values, member)


def seg_at(starts_ref, positions):
    total = jnp.zeros(positions.shape, jnp.int32)
    for j in range(starts_ref.shape[0]):
        total = total + jnp.where(positions >= starts_ref[j], 1, 0)
    return total


def scalar_seg(starts_ref, position):
    total = jnp.int32(0)
    for j in range(starts_ref.shape[0]):
        total = total + jnp.where(position >= starts_ref[j], 1, 0)
    return total


def row_positions(base, rows):
    return base + lax.broadcasted_iota(jnp.int32, (rows, LANES), 0)


def pair_mask(starts_ref, base, rows, transposed):
    down = lax.broadcasted_iota(jnp.int32, (rows, rows), 0)
    across = lax.broadcasted_iota(jnp.int32, (rows, rows), 1)
    seg_down = seg_at(starts_ref, base + lax.broadcasted_iota(jnp.int32, (rows, LANES), 0))
    seg_down = jnp.concatenate([seg_down] * (rows // LANES), axis=1)
    seg_across = seg_at(starts_ref, base + lax.broadcasted_iota(jnp.int32, (8, rows), 1))
    order = down <= across if transposed else down >= across
    return jnp.where(order & (seg_down == seg_across[0:1, :]), 0.0, FAR)


def enter_of(starts_ref, base, cumulative):
    rows = cumulative.shape[0]
    alive = seg_at(starts_ref, row_positions(base, rows)) == scalar_seg(starts_ref, base - 1)
    return jnp.where(alive, jnp.exp(cumulative), 0.0)


def tail_of(starts_ref, base, cumulative):
    rows = cumulative.shape[0]
    same = seg_at(starts_ref, row_positions(base, rows)) == scalar_seg(starts_ref, base + rows - 1)
    return jnp.where(same, jnp.exp(cumulative[rows - 1 : rows, :] - cumulative), 0.0)


def sigmoid(value):
    return 1.0 / (1.0 + jnp.exp(-value))


def silu(value):
    return value * sigmoid(value)


def states_kernel(
    starts, x_ref, bc_ref, step_ref, cum_ref, enter_o, prefix_o, final_o, total_o, state, passed,
    *, head_width, parts,
):
    rows, inner = x_ref.shape
    state_width = bc_ref.shape[1] // 2
    block = pl.program_id(0)
    base = block * rows

    @pl.when(block == 0)
    def _():
        state[...] = jnp.zeros_like(state)
        passed[...] = jnp.ones_like(passed)

    cumulative = cum_ref[...]
    enter = enter_of(starts, base, cumulative)
    tail = tail_of(starts, base, cumulative)
    before = passed[0:1, :]
    prefix_o[0] = jnp.broadcast_to(before, prefix_o.shape[1:])
    enter_o[0] = state[...]
    after = before * enter[rows - 1 : rows, :]
    passed[...] = jnp.broadcast_to(after, passed.shape)
    total_o[...] = jnp.broadcast_to(after, total_o.shape)

    scaled = x_ref[...].astype(F32) * spread_heads(step_ref[...], inner, head_width)
    tailed = split(scaled * spread_heads(tail, inner, head_width), parts)
    added = sum_dots(t_dot, [bc_ref[:, :state_width]], tailed)
    end = spread_heads(enter[rows - 8 : rows, :], inner, head_width)[7:8, :]
    new_state = state[...] * end + added
    state[...] = new_state
    final_o[...] = new_state


def within_kernel(starts, x_ref, bc_ref, step_ref, cum_ref, skip_ref, y_o, *, head_width, parts):
    rows, inner = x_ref.shape
    state_width = bc_ref.shape[1] // 2
    base = pl.program_id(0) * rows
    x = x_ref[...].astype(F32)
    scaled = split(x * spread_heads(step_ref[...], inner, head_width), parts)
    scores = dot_t(bc_ref[:, state_width:], bc_ref[:, :state_width])
    mask = pair_mask(starts, base, rows, False)
    cumulative = cum_ref[...]
    across = cumulative.T
    lane = lax.broadcasted_iota(jnp.int32, (rows, LANES), 1)
    for start, width in lane_chunks(inner):
        total = None
        for k in range(width // head_width):
            head = start // head_width + k
            spread = cumulative[:, head : head + 1] - across[head : head + 1, :]
            mixing = split(jnp.exp(spread + mask) * scores, parts)
            part = sum_dots(dot, mixing, [piece[:, start : start + width] for piece in scaled])
            if total is None:
                total = part
            else:
                total = jnp.where(lane[:, :width] >= k * head_width, part, total)
        lanes = slice(start, start + width)
        y_o[:, lanes] = total + skip_ref[:, lanes] * x[:, lanes]


def close_kernel(
    starts, y_ref, bc_ref, cum_ref, enter_ref, prefix_ref, chain_ref, gate_ref, gain_ref, w_ref,
    mixed_o, state_o, rest_o, square_o, *terms_o,
    head_width, parts,
):
    rows, inner = y_ref.shape
    state_width = bc_ref.shape[1] // 2
    base = pl.program_id(0) * rows
    entering = enter_ref[0] + spread_heads(prefix_ref[0], inner, head_width)[0:1, :] * chain_ref[...]
    pieces = split(entering, parts)
    state_o[0] = pieces[0]
    rest_o[0] = pieces[1]
    enter = spread_heads(enter_of(starts, base, cum_ref[...]), inner, head_width)
    c_proj = bc_ref[:, state_width:]
    mixed = y_ref[...] + enter * sum_dots(dot, [c_proj], pieces)
    mixed_o[...] = mixed
    gated = mixed * silu(gate_ref[...].astype(F32))
    square = jnp.broadcast_to(jnp.sum(gated * gated, axis=1, keepdims=True), (rows, LANES))
    square_o[0] = square.T[0:8, :]
    for ref in terms_o:
        ref[...] = dot((gated * gain_ref[...]).astype(BF), w_ref[...]).astype(ref.dtype)


def out_kernel(mixed_ref, gate_ref, inv_ref, gain_ref, w_ref, terms_o):
    gated = mixed_ref[...] * silu(gate_ref[...].astype(F32))
    terms_o[...] = dot((gated * inv_ref[...] * gain_ref[...]).astype(BF), w_ref[...])


def dots_kernel(grad_ref, w_ref, gain_ref, gate_ref, mixed_ref, dots_o):
    d_normed = dot_t(grad_ref[...].astype(BF), w_ref[...])
    gated = mixed_ref[...] * silu(gate_ref[...].astype(F32))
    total = jnp.sum(d_normed * gain_ref[...] * gated, axis=1, keepdims=True)
    dots_o[0] = jnp.broadcast_to(total, (total.shape[0], LANES)).T[0:8, :]


def open_kernel(
    starts, grad_ref, total_ref, inv_ref, w_ref, gain_ref, gate_ref, mixed_ref, bc_ref, cum_ref, unit_ref,
    d_gate_o, dy_o, grad_out_o, grad_gate_o, grad_mix_o, chain_o,
    carry,
    *, head_width, inner_all,
):
    rows, inner = mixed_ref.shape
    state_width = bc_ref.shape[1] // 2
    step_id = pl.program_id(0)
    block = pl.num_programs(0) - 1 - step_id
    base = block * rows

    @pl.when(step_id == 0)
    def _():
        carry[...] = jnp.zeros_like(carry)
        grad_out_o[...] = jnp.zeros_like(grad_out_o)
        grad_mix_o[...] = jnp.zeros_like(grad_mix_o)
        grad_gate_o[...] = jnp.zeros_like(grad_gate_o)

    inv = inv_ref[...]
    low = grad_ref[...].astype(BF)
    total_dot = total_ref[...]
    d_normed = dot_t(low, w_ref[...])
    gate = gate_ref[...].astype(F32)
    sig = sigmoid(gate)
    act = gate * sig
    mixed = mixed_ref[...]
    gated = mixed * act
    gain = gain_ref[...]
    unit = gated * inv
    grad_mix_o[...] += jnp.sum(d_normed * unit, axis=0, keepdims=True)
    grad_out_o[...] += t_dot((unit * gain).astype(BF), low)
    cube = inv * inv * inv
    d_gated = inv * (d_normed * gain) - gated * (cube * total_dot * (1.0 / inner_all))
    dy = d_gated * act
    dy_o[...] = dy
    d_gate = (d_gated * mixed * sig * (1.0 + gate * (1.0 - sig))).astype(BF)
    d_gate_o[...] = d_gate
    grad_gate_o[...] += t_dot(unit_ref[...], d_gate)

    enter = spread_heads(enter_of(starts, base, cum_ref[...]), inner, head_width)
    entered = split(dy * enter)
    new = carry[...] * enter[rows - 1 : rows, :] + sum_dots(t_dot, [bc_ref[:, state_width:]], entered)
    carry[...] = new
    chain_o[...] = new


def within_back_kernel(
    starts, x_ref, bc_ref, step_ref, cum_ref, dy_ref, d_scaled_o, d_bc_o, *, head_width
):
    rows, inner = x_ref.shape
    state_width = bc_ref.shape[1] // 2
    base = pl.program_id(0) * rows
    scaled = x_ref[...].astype(F32) * spread_heads(step_ref[...], inner, head_width)
    b_proj = bc_ref[:, :state_width]
    c_proj = bc_ref[:, state_width:]
    scores = dot_t(b_proj, c_proj)
    mask = pair_mask(starts, base, rows, True)
    cumulative = cum_ref[...]
    across = cumulative.T
    lane = lax.broadcasted_iota(jnp.int32, (rows, LANES), 1)
    d_scores = jnp.zeros((rows, rows), F32)
    for start, width in lane_chunks(inner):
        lanes = slice(start, start + width)
        dy, dy_rest = split(dy_ref[:, lanes])
        wide = scaled[:, lanes]
        total = None
        for k in range(width // head_width):
            head = start // head_width + k
            spread = across[head : head + 1, :] - cumulative[:, head : head + 1]
            decay = jnp.exp(spread + mask)
            part = sum_dots(dot, split(decay * scores), [dy, dy_rest])
            inside = (lane >= k * head_width) & (lane < (k + 1) * head_width)
            one = split(jnp.where(inside[:, :width], wide, 0.0))
            d_scores = d_scores + sum_dots(dot_t, one, [dy, dy_rest]) * decay
            if total is None:
                total = part
            else:
                total = jnp.where(lane[:, :width] >= k * head_width, part, total)
        d_scaled_o[:, lanes] = total
    d_scores = split(d_scores)
    d_bc_o[:, :state_width] = sum_dots(dot, d_scores, [c_proj])
    d_bc_o[:, state_width:] = sum_dots(t_dot, d_scores, [b_proj])


def finish_kernel(
    starts, x_ref, bc_ref, step_ref, cum_ref, dy_ref, mixed_ref, state_ref, rest_ref, d_scaled_ref, d_bc_ref,
    conv_v, conv_s, pre_ref, state_pre_ref, d_gate_ref, unit_ref, h_ref, from_later, skip_ref, neg_rate,
    taps_v, taps_s, w_ref,
    d_unit_o, grad_w_o, small_o, first_v_o, first_s_o,
    carry, ext_v, ext_s, d_all, d_rest,
    *, head_width, margin,
):
    rows, inner = x_ref.shape
    wide = up(inner)
    state2 = bc_ref.shape[1]
    state_width = state2 // 2
    step_id = pl.program_id(0)
    block = pl.num_programs(0) - 1 - step_id
    base = block * rows

    @pl.when(step_id == 0)
    def _():
        carry[...] = from_later[...]
        for ref in (grad_w_o, small_o, d_all):
            ref[...] = jnp.zeros_like(ref)
        ext_v[rows : rows + 8, :] = jnp.zeros((8, inner), F32)
        ext_s[rows : rows + 8, :] = jnp.zeros((8, state2), F32)

    x = x_ref[...].astype(F32)
    dy = dy_ref[...]
    b_proj = bc_ref[:, :state_width]
    c_proj = bc_ref[:, state_width:]
    step = step_ref[...]
    steps = spread_heads(step, inner, head_width)
    scaled = x * steps
    cumulative = cum_ref[...]
    enter = spread_heads(enter_of(starts, base, cumulative), inner, head_width)
    tail = spread_heads(tail_of(starts, base, cumulative), inner, head_width)
    skip = skip_ref[...]
    queue = carry[...]
    state = state_ref[0]
    end = enter[rows - 1 : rows, :]
    entered = split(dy * enter)

    queues = split(queue)
    d_inter = tail * sum_dots(dot, [b_proj], queues)
    d_b = sum_dots(dot_t, split(tail * scaled), queues) + d_bc_ref[:, :state_width]
    d_c = sum_dots(dot_t, entered, [state, rest_ref[0]]) + d_bc_ref[:, state_width:]
    carry[...] = queue * end + sum_dots(t_dot, [c_proj], entered)
    d_scaled = d_scaled_ref[...] + d_inter
    d_x = steps * d_scaled + skip * dy
    small_o[5:6, :inner] += jnp.sum(x * dy, axis=0, keepdims=True)
    d_step = head_sums(x * d_scaled, head_width)
    d_cum = head_sums(dy * (mixed_ref[...] - skip * x) - scaled * d_scaled, head_width)
    leaving = jnp.sum(scaled * d_inter, axis=0, keepdims=True) + end * jnp.sum(
        queue * state.astype(F32), axis=0, keepdims=True
    )
    leaving = head_sums(jnp.broadcast_to(leaving, (8, inner)), head_width)[0:1, :]
    down = lax.broadcasted_iota(jnp.int32, (rows, rows), 0)
    across = lax.broadcasted_iota(jnp.int32, (rows, rows), 1)
    d_rate = dot_high(jnp.where(down <= across, 1.0, 0.0), d_cum) + leaving
    d_raw = (d_step + neg_rate[...] * d_rate) * (1.0 - jnp.exp(-step))
    small_o[6:7, :LANES] += jnp.sum(d_raw, axis=0, keepdims=True)
    small_o[7:8, :LANES] += jnp.sum(d_rate * step * neg_rate[...], axis=0, keepdims=True)

    positions = row_positions(base, rows)
    seg_here = seg_at(starts, positions)
    masks = [
        jnp.where(seg_at(starts, positions + j) == seg_here, 1.0, 0.0) for j in range(1, margin + 1)
    ]
    d_all[:, :inner] = d_gate_ref[...]
    d_post_s = jnp.concatenate([d_b, d_c], axis=1)
    for d_post, conv, ext, first_o, in_ref, taps, row, place in (
        (d_x, conv_v, ext_v, first_v_o, pre_ref, taps_v, 0, wide),
        (d_post_s, conv_s, ext_s, first_s_o, state_pre_ref, taps_s, 8, 2 * wide),
    ):
        for start, width in lane_chunks(ext.shape[1]):
            lanes = slice(start, start + width)
            value = conv[:, lanes]
            sig = sigmoid(value)
            d_conv = d_post[:, lanes] * sig * (1.0 + value * (1.0 - sig))
            ext[0:rows, lanes] = d_conv
            last = row + margin
            small_o[last + 1 : last + 2, lanes] += jnp.sum(d_conv, axis=0, keepdims=True)
            source = in_ref[:, lanes].astype(F32)
            total = taps[margin : margin + 1, lanes] * d_conv
            small_o[last : last + 1, lanes] += jnp.sum(source * d_conv, axis=0, keepdims=True)
            for j in range(1, margin + 1):
                moved = ext[j : j + rows, lanes] * masks[j - 1][:, :width]
                total = total + taps[margin - j : margin - j + 1, lanes] * moved
                small_o[last - j : last - j + 1, lanes] += jnp.sum(source * moved, axis=0, keepdims=True)
            low, rest = split(total)
            d_all[:, place + start : place + start + width] = low
            if ext is ext_s:
                d_rest[:, lanes] = rest
        first_o[...] = ext[0:8, :]
        ext[rows : rows + 8, :] = ext[0:8, :]
    d_all[:, 2 * wide + state2 :] = d_raw.astype(BF)
    d_low = d_all[...]
    unit = unit_ref[...]
    d_unit = dot_t(d_low, w_ref[...]) + dot_t(d_rest[...], w_ref[:, 2 * wide : 2 * wide + state2])
    d_unit_o[...] = d_unit
    grad_w_o[...] += t_dot(unit, d_low[:, wide:])
    grad_w_o[:, wide : wide + state2] += t_dot(unit, d_rest[...])
    h = h_ref[...]
    scale = lax.rsqrt(jnp.mean(h * h, axis=-1, keepdims=True) + EPS)
    small_o[13:14, :] += jnp.sum(d_unit * (h * scale), axis=0, keepdims=True)


def shape_of(shape, dtype):
    return jax.ShapeDtypeStruct(shape, dtype)


SCALARS = pl.BlockSpec(memory_space=pltpu.SMEM)


def whole_spec(shape):
    return pl.BlockSpec(shape, lambda i: (0,) * len(shape))


def call(body, name, blocks, ins, outs, scratch, flops, backward=False, **fixed):
    def place(i):
        return blocks - 1 - i if backward else i

    def spec(shape, kind):
        if kind == "scalars":
            return SCALARS
        if kind == "rows":
            return pl.BlockSpec((shape[0] // blocks, shape[1]), lambda i: (place(i), 0))
        if kind == "block":
            return pl.BlockSpec((1,) + shape[1:], lambda i: (place(i), 0, 0))
        return whole_spec(shape)

    moved = sum(array.size * array.dtype.itemsize for array, _ in ins)
    moved += sum(size_of(shape) * jnp.dtype(dtype).itemsize for shape, dtype, _ in outs)
    return pl.pallas_call(
        partial(body, **fixed),
        name=name,
        grid=(blocks,),
        in_specs=[spec(array.shape, kind) for array, kind in ins],
        out_specs=[spec(shape, kind) for shape, _, kind in outs],
        out_shape=[shape_of(shape, dtype) for shape, dtype, _ in outs],
        scratch_shapes=scratch,
        cost_estimate=pl.CostEstimate(flops=flops // 1, bytes_accessed=moved // 1, transcendentals=0),
        compiler_params=pltpu.CompilerParams(vmem_limit_bytes=48 * 1024 * 1024),
    )(*[array for array, _ in ins])


def size_of(shape):
    total = 1
    for extent in shape:
        total *= extent
    return total


def shift(block, axis, distance):
    devices = range(lax.axis_size(axis))
    return lax.ppermute(block, axis, [(i - distance, i) for i in devices if i - distance in devices])


def carried_state(decay, state, reverse):
    count = lax.axis_size("seq")
    sign = -1 if reverse else 1
    distance = 1
    rows = state.shape[0]
    before_state = None
    while distance < count:
        packed = jnp.concatenate([state, jnp.broadcast_to(decay, (8, state.shape[1]))], axis=0)
        packed = shift(packed, "seq", sign * distance)
        got_state, got_decay = packed[:rows], packed[rows : rows + 1]
        if before_state is None:
            before_state, before_decay = got_state, got_decay
        else:
            before_state = before_decay * got_state + before_state
            before_decay = before_decay * got_decay
        if 2 * distance < count:
            state = decay * got_state + state
            decay = decay * got_decay
        distance *= 2
    return before_state


def sum_heads(terms, wire):
    count = lax.axis_size("head")
    kind = terms.dtype
    if count != 4:
        return lax.psum(terms, "head")
    core = lax.axis_index("head") % 2
    half = terms.shape[0] // 2
    siblings = [(i, i ^ 1) for i in range(count)]
    mine = lax.dynamic_slice_in_dim(terms, core * half, half, 0)
    other = lax.dynamic_slice_in_dim(terms, (1 - core) * half, half, 0)
    part = mine.astype(F32) + lax.ppermute(other, "head", siblings).astype(F32)
    part = part.astype(wire)
    across = lax.ppermute(part, "head", [(i, i ^ 2) for i in range(count)])
    part = (part.astype(F32) + across.astype(F32)).astype(kind)
    back = lax.ppermute(part, "head", siblings)
    return jnp.where(
        core == 0, jnp.concatenate([part, back], axis=0), jnp.concatenate([back, part], axis=0)
    )


def sum_small(value):
    count = lax.axis_size("head")
    if count != 4:
        return lax.psum(value, "head")
    value = value + lax.ppermute(value, "head", [(i, i ^ 1) for i in range(count)])
    return value + lax.ppermute(value, "head", [(i, i ^ 2) for i in range(count)])


def padded(array, width):
    return jnp.pad(array, ((0, 0), (0, width - array.shape[1])))


def local(
    hidden,
    doc_starts,
    norm_gain,
    w_gate,
    w_value,
    w_state,
    w_step,
    conv_value,
    conv_state,
    bias_value,
    bias_state,
    step_bias,
    a_log,
    skip_gain,
    mix_gain,
    w_out,
    cotangent,
):
    tokens, model = hidden.shape
    layer_count = norm_gain.shape[0]
    inner = w_gate.shape[2]
    heads = w_step.shape[2]
    inner_all = inner * lax.axis_size("head")
    head_width = inner // heads
    state2 = w_state.shape[2]
    state_width = state2 // 2
    margin = conv_value.shape[1] - 1
    blocks = tokens // GROUP
    wide = up(inner)
    total_wide = 2 * wide + state2 + LANES
    starts = doc_starts.astype(jnp.int32) - lax.axis_index("seq") * tokens

    def vmem(*shape, dtype=F32):
        return pltpu.VMEM(shape, dtype)

    positions = jnp.arange(-margin, tokens)
    seg_pad = jnp.sum((starts[None, :] <= positions[:, None]).astype(jnp.int32), axis=1)
    weights, fixed = [], []
    for layer in range(layer_count):
        weights.append(
            jnp.concatenate(
                [
                    padded(w_gate[layer], wide),
                    padded(w_value[layer], wide),
                    w_state[layer],
                    padded(w_step[layer], LANES),
                ],
                axis=1,
            )
        )
        fixed.append(
            (
                padded(-jnp.exp(a_log[layer])[None, :], LANES),
                jnp.repeat(skip_gain[layer], head_width)[None, :],
            )
        )
    project_flops = 2 * tokens * model * total_wide
    out_flops = 2 * tokens * inner * model
    within_flops = 2 * tokens * GROUP * (LANES * heads + state_width)

    def lanes_of(decay):
        return jnp.repeat(decay[0:1, :heads], head_width, axis=1)

    current = hidden
    records = []
    for layer in range(layer_count):
        skip = fixed[layer][1]
        last_layer = layer == layer_count - 1
        parts = 3
        unit = (rms_scale(current) * norm_gain[layer][None, :]).astype(BF)
        proj = dot(unit, weights[layer]).astype(BF)
        gate = proj[:, :inner]
        pre = proj[:, wide : wide + inner]
        state_pre = proj[:, 2 * wide : 2 * wide + state2]
        raw = proj[:, 2 * wide + state2 : 2 * wide + state2 + heads].astype(F32)
        halo = jnp.concatenate([pre[tokens - margin :], state_pre[tokens - margin :]], axis=1)
        halo = shift(halo, "seq", 1)
        conv_v = causal_conv(
            jnp.concatenate([halo[:, :inner], pre], axis=0).astype(F32),
            seg_pad,
            conv_value[layer],
            bias_value[layer],
        )
        conv_s = causal_conv(
            jnp.concatenate([halo[:, inner:], state_pre], axis=0).astype(F32),
            seg_pad,
            conv_state[layer],
            bias_state[layer],
        )
        x = jax.nn.silu(conv_v).astype(BF)
        bc = jax.nn.silu(conv_s).astype(BF)
        step = jax.nn.softplus(raw + step_bias[layer][None, :])
        rate = -step * jnp.exp(a_log[layer])[None, :]
        cum = jnp.cumsum(rate.reshape(blocks, GROUP, heads), axis=1).reshape(tokens, heads)
        step = padded(step, LANES)
        cum = padded(cum, LANES)
        enter_state, prefix, final, total = call(
            states_kernel,
            "states",
            blocks,
            [(starts, "scalars"), (x, "rows"), (bc, "rows"), (step, "rows"), (cum, "rows")],
            [
                ((blocks, state_width, inner), F32, "block"),
                ((blocks, 8, LANES), F32, "block"),
                ((state_width, inner), F32, "whole"),
                ((8, LANES), F32, "whole"),
            ],
            [vmem(state_width, inner), vmem(8, LANES)],
            2 * tokens * inner * state_width,
            head_width=head_width,
            parts=parts,
        )
        (within,) = call(
            within_kernel,
            "within",
            blocks,
            [(starts, "scalars"), (x, "rows"), (bc, "rows"), (step, "rows"), (cum, "rows"), (skip, "whole")],
            [((tokens, inner), F32, "rows")],
            [],
            within_flops,
            head_width=head_width,
            parts=parts,
        )
        decay_total = lanes_of(total)
        chain_in = carried_state(decay_total, final, False)
        mixed, state_in, state_rest, square, *terms = call(
            close_kernel,
            "close",
            blocks,
            [
                (starts, "scalars"),
                (within, "rows"),
                (bc, "rows"),
                (cum, "rows"),
                (enter_state, "block"),
                (prefix, "block"),
                (chain_in, "whole"),
                (gate, "rows"),
                (mix_gain[layer][None, :], "whole"),
                (w_out[layer], "whole"),
            ],
            [
                ((tokens, inner), F32, "rows"),
                ((blocks, state_width, inner), BF, "block"),
                ((blocks, state_width, inner), BF, "block"),
                ((blocks, 8, GROUP), F32, "block"),
            ]
            + [((tokens, model), BF, "rows")] * last_layer,
            [],
            out_flops,
            head_width=head_width,
            parts=parts,
        )
        square = sum_small(square[:, 0, :])
        inv = lax.rsqrt(square * (1.0 / inner_all) + EPS).reshape(tokens, 1)
        if last_layer:
            summed = sum_heads(terms[0], BF)
            following = current + inv * summed.astype(F32)
        else:
            (out,) = call(
                out_kernel,
                "out",
                blocks,
                [
                    (mixed, "rows"),
                    (gate, "rows"),
                    (inv, "rows"),
                    (mix_gain[layer][None, :], "whole"),
                    (w_out[layer], "whole"),
                ],
                [((tokens, model), F32, "rows")],
                [],
                out_flops,
            )
            summed = sum_heads(out, F32)
            following = current + summed
        records.append(
            (current, unit, gate, pre, state_pre, conv_v, conv_s, x, bc, step, cum, mixed, (state_in, state_rest), inv, decay_total)
        )
        current = following

    grad = cotangent
    totals = [None] * layer_count
    sums = []
    for layer in reversed(range(layer_count)):
        neg_rate, skip = fixed[layer]
        (h_in, unit, gate, pre, state_pre, conv_v, conv_s, x, bc, step, cum, mixed, state_in, inv, decay_total) = records[layer]
        (dots,) = call(
            dots_kernel,
            "dots",
            blocks,
            [
                (grad, "rows"),
                (w_out[layer], "whole"),
                (mix_gain[layer][None, :], "whole"),
                (gate, "rows"),
                (mixed, "rows"),
            ],
            [((blocks, 8, GROUP), F32, "block")],
            [],
            out_flops,
        )
        total_dot = sum_small(dots[:, 0, :]).reshape(tokens, 1)
        d_gate, dy, grad_out, grad_gate, grad_mix, grad_chain = call(
            open_kernel,
            "open",
            blocks,
            [
                (starts, "scalars"),
                (grad, "rows"),
                (total_dot, "rows"),
                (inv, "rows"),
                (w_out[layer], "whole"),
                (mix_gain[layer][None, :], "whole"),
                (gate, "rows"),
                (mixed, "rows"),
                (bc, "rows"),
                (cum, "rows"),
                (unit, "rows"),
            ],
            [
                ((tokens, inner), BF, "rows"),
                ((tokens, inner), F32, "rows"),
                ((inner, model), F32, "whole"),
                ((model, inner), F32, "whole"),
                ((1, inner), F32, "whole"),
                ((state_width, inner), F32, "whole"),
            ],
            [vmem(state_width, inner)],
            2 * out_flops,
            backward=True,
            head_width=head_width,
            inner_all=inner_all,
        )
        d_scaled, d_bc = call(
            within_back_kernel,
            "within_back",
            blocks,
            [(starts, "scalars"), (x, "rows"), (bc, "rows"), (step, "rows"), (cum, "rows"), (dy, "rows")],
            [((tokens, inner), F32, "rows"), ((tokens, state2), F32, "rows")],
            [],
            2 * within_flops,
            head_width=head_width,
        )
        early = (grad_gate.astype(BF), grad_out.astype(BF))
        if sums:
            early, _ = lax.optimization_barrier((early, sums[-1]))
        early = lax.psum(early, "seq")
        from_later = carried_state(decay_total, grad_chain, True)
        if sums:
            from_later, sums[-1] = lax.optimization_barrier((from_later, sums[-1]))
        (
            d_unit, grad_w, small, first_v, first_s,
        ) = call(
            finish_kernel,
            "finish",
            blocks,
            [
                (starts, "scalars"),
                (x, "rows"),
                (bc, "rows"),
                (step, "rows"),
                (cum, "rows"),
                (dy, "rows"),
                (mixed, "rows"),
                (state_in[0], "block"),
                (state_in[1], "block"),
                (d_scaled, "rows"),
                (d_bc, "rows"),
                (conv_v, "rows"),
                (conv_s, "rows"),
                (pre, "rows"),
                (state_pre, "rows"),
                (d_gate, "rows"),
                (unit, "rows"),
                (h_in, "rows"),
                (from_later, "whole"),
                (skip, "whole"),
                (neg_rate, "whole"),
                (conv_value[layer], "whole"),
                (conv_state[layer], "whole"),
                (weights[layer], "whole"),
            ],
            [
                ((tokens, model), F32, "rows"),
                ((model, total_wide - wide), F32, "whole"),
                ((16, model), F32, "whole"),
                ((8, inner), F32, "whole"),
                ((8, state2), F32, "whole"),
            ],
            [
                vmem(state_width, inner),
                vmem(GROUP + 8, inner),
                vmem(GROUP + 8, state2),
                vmem(GROUP, total_wide, dtype=BF),
                vmem(GROUP, state2, dtype=BF),
            ],
            2 * project_flops,
            backward=True,
            head_width=head_width,
            margin=margin,
        )
        first = jnp.concatenate([first_v, first_s], axis=1)
        from_next = shift(first, "seq", -1)
        taps = jnp.concatenate([conv_value[layer], conv_state[layer]], axis=1)
        source = jnp.concatenate([pre[tokens - 8 :], state_pre[tokens - 8 :]], axis=1).astype(F32)
        rows8 = jnp.arange(tokens - 8, tokens)

        def segs(positions):
            return jnp.sum((starts[None, :] <= positions[:, None]).astype(jnp.int32), axis=1)

        padded_next = jnp.concatenate([jnp.zeros_like(from_next), from_next], axis=0)
        extra = jnp.zeros_like(from_next)
        extra_taps = [jnp.zeros((inner + state2,), F32)] * (margin + 1)
        for j in range(1, margin + 1):
            same = (segs(rows8 + j) == segs(rows8)).astype(F32)[:, None]
            moved = padded_next[j : j + 8] * same
            extra = extra + taps[margin - j][None, :] * moved
            extra_taps[margin - j] = jnp.sum(source * moved, axis=0)
        extra_taps = jnp.stack(extra_taps)
        extra_low = extra.astype(BF)
        w_conv = jnp.concatenate([w_value[layer], w_state[layer]], axis=1)
        extra_unit = dot_t(extra_low, w_conv)
        extra_w = t_dot(unit[tokens - 8 :], extra_low)
        d_unit = jnp.concatenate(
            [d_unit[: tokens - 8], d_unit[tokens - 8 :] + extra_unit], axis=0
        )
        last = h_in[tokens - 8 :]
        last = last * lax.rsqrt(jnp.mean(last * last, axis=-1, keepdims=True) + EPS)
        zeros = jnp.zeros((4, model), F32)
        extra_small = jnp.concatenate(
            [
                padded(extra_taps[:, :inner], model),
                zeros,
                padded(extra_taps[:, inner:], model),
                zeros[:1],
                jnp.sum(extra_unit * last, axis=0)[None, :],
                zeros[:2],
            ],
            axis=0,
        )
        small = jnp.concatenate(
            [small + extra_small, padded(grad_mix, model), jnp.zeros((15, model), F32)], axis=0
        )
        small = small.reshape(32 * model // state2, state2)
        extra_w = jnp.concatenate(
            [padded(extra_w[:, :inner], wide), extra_w[:, inner:], jnp.zeros((model, LANES), F32)], axis=1
        )
        grad_w = grad_w + extra_w
        late = jnp.concatenate([grad_w[:, :wide], grad_w[:, wide + state2 :]], axis=1).astype(BF)
        late = (late, jnp.concatenate([grad_w[:, wide : wide + state2], small], axis=0))
        d_unit, late, early = lax.optimization_barrier((d_unit, late, early))
        late = lax.psum(late, "seq")
        sums.append(late)
        late_small = late[1][model:].reshape(32, model)
        d_total = sum_heads(d_unit, F32)
        scale = lax.rsqrt(jnp.mean(h_in * h_in, axis=-1, keepdims=True) + EPS)
        gained = d_total * norm_gain[layer][None, :]
        inner_dot = jnp.mean(gained * h_in, axis=-1, keepdims=True)
        grad = grad + scale * gained - h_in * (scale * scale * scale * inner_dot)

        totals[layer] = early + (late[0], late_small, late[1][:model])
    stated = [totals[layer][4] for layer in range(layer_count)]
    stated = sum_heads(jnp.concatenate(stated, axis=0), F32)
    smalls = jnp.stack([totals[layer][3] for layer in range(layer_count)])
    shared = sum_small(smalls[:, 8:16, :])
    gate_g, out_g, late_g = (
        jnp.stack([totals[layer][member] for layer in range(layer_count)]).astype(F32)
        for member in range(3)
    )
    taps = margin + 1
    return (
        current,
        grad,
        shared[:, 5],
        gate_g,
        late_g[:, :, :inner],
        stated.reshape(layer_count, model, state2),
        late_g[:, :, wide : wide + heads],
        smalls[:, :taps, :inner],
        shared[:, :taps, :state2],
        smalls[:, taps, :inner],
        shared[:, taps, :state2],
        smalls[:, 6, :heads],
        smalls[:, 7, :heads],
        jnp.sum(smalls[:, 5, :inner].reshape(layer_count, heads, head_width), axis=2),
        smalls[:, 16, :inner],
        out_g,
    )


def solution(mesh):
    return jax.shard_map(
        local,
        mesh=mesh,
        in_specs=(
            P("seq", None),
            P(),
            P(),
            P(None, None, "head"),
            P(None, None, "head"),
            P(),
            P(None, None, "head"),
            P(None, None, "head"),
            P(),
            P(None, "head"),
            P(),
            P(None, "head"),
            P(None, "head"),
            P(None, "head"),
            P(None, "head"),
            P(None, "head", None),
            P("seq", None),
        ),
        out_specs=(
            P("seq", None),
            P("seq", None),
            P(),
            P(None, None, "head"),
            P(None, None, "head"),
            P(),
            P(None, None, "head"),
            P(None, None, "head"),
            P(),
            P(None, "head"),
            P(),
            P(None, "head"),
            P(None, "head"),
            P(None, "head"),
            P(None, "head"),
            P(None, "head", None),
        ),
        check_vma=False,
    )
```
